256 devices in a mesh: node: 4 (over x), row: 64 (over y, z, core).
Axes of the slice: x: 4, y: 4, z: 8, core: 2. Of those that a mesh axis runs over, the one named last changes fastest.
Arguments:
- front_slab: bfloat16 [8192, 122880], P('node', 'row'), may hold values from -0.046875 to 0.046875
- omega_codes: int32 [122880, 384], P('row'), may hold values from -3 to 3
- block_mask: int32 [32, 192], P('node', 'row'), may hold values 0 or 1
- leaf_pivots: int32 [4, 128], P('node'), may hold values from 0 to 2047, as said below
- mid_pivots: int32 [2, 128], replicated, may hold values from 0 to 255, as said below
- root_pivots: int32 [128], replicated, may hold values from 0 to 255, as said below
Outputs:
- leaf_interp: float32 [8192, 128], P(('node', 'row'))
- mid_interp: float32 [512, 128], P('node')
- root_interp: float32 [256, 128], P('node')
- root_skeleton: float32 [128, 384], replicated
The draws below stay inside these ranges and needn't reach their ends.
Inputs may be any that keep to these rules, and one draw needn't show every extreme that they name: `leaf_pivots`: each row holds 128 different row numbers of its subtree, 0 and 2047 among them. `mid_pivots`: each row holds 128 different positions among the 256 stacked child skeleton rows, 0 and 255 among them. `root_pivots`: 128 different positions among the 256 stacked middle skeleton rows, 0 and 255 among them.
All inputs are finite; a program needn't handle non-finite values. No bound on the sum of `block_mask` on one device may be relied on, other than what follows from the above.
Results may differ from the reference program's by a relative error of at most 0.0003.
Values sent between devices are 32-bit elements; how exact they have to be, the bound alone decides.
A program may use at most 128 MiB of HBM per device.

```python
import jax
import jax.numpy as jnp
from jax import lax

N = 122880
MS = 2048
K = 128
R = 384
BR = 256
BC = 640
NODES = 4
M = 8192
MB = 32
NB = 192


def pick_rows(key, total, wanted):
    inner = jax.random.permutation(key, total - 2)[:wanted - 2] + 1
    chosen = jnp.concatenate([inner.astype(jnp.int32), jnp.array([0, total - 1], jnp.int32)])
    order = jax.random.permutation(jax.random.fold_in(key, 7), wanted)
    return chosen[order].astype(jnp.int32)


def draw_leaf_pivots(key, part):
    key = jax.random.fold_in(key, 11)
    keys = jax.random.split(key, NODES)
    return jax.vmap(lambda sub_key: pick_rows(sub_key, MS, K))(keys)


def draw_mid_pivots(key, part):
    key = jax.random.fold_in(key, 23)
    keys = jax.random.split(key, NODES // 2)
    return jax.vmap(lambda sub_key: pick_rows(sub_key, 2 * K, K))(keys)


def draw_root_pivots(key, part):
    key = jax.random.fold_in(key, 37)
    return pick_rows(key, 2 * K, K)


def touch_ends(entries, rng, smallest, top_value):
    longest = entries.shape.index(max(entries.shape))
    spots = []
    for shift in (0, 1):
        where = [jax.random.randint(jax.random.fold_in(rng, axis), (), 0, length) for axis, length in enumerate(entries.shape)]
        where[longest] = (where[longest] + shift) % entries.shape[longest]
        spots.append(tuple(where))
    return entries.at[spots[0]].set(smallest).at[spots[1]].set(top_value)


def strengthened(drawn, stream_key, source, target, blocks, factor):
    def block_of(position):
        return (jnp.arange(drawn.shape[position]) // (drawn.shape[position] // blocks)).reshape((-1,) + (1,) * (drawn.ndim - 1 - position))

    near = jax.random.permutation(stream_key, blocks)[block_of(target)]
    far = (block_of(target) + blocks // 2) % blocks
    return jnp.where((block_of(source) == near) | (block_of(source) == far), factor * drawn, drawn)


def level_of(stream_key, extent, cuts, least, high):
    def one(axis_at, parts):
        steps = jax.random.uniform(jax.random.fold_in(jax.random.fold_in(stream_key, 6), axis_at), (parts,), jnp.float32, least / len(cuts), high / len(cuts))
        return jnp.repeat(jnp.exp(steps), extent[axis_at] // parts).reshape((-1,) + (1,) * (len(extent) - axis_at - 1))

    gain = one(*cuts[0])
    for cut in cuts[1:]:
        gain = gain * one(*cut)
    return gain


def heavy_noise(stream_key, extent, spread, reach, cuts, heavy, held_as=jnp.bfloat16):
    values = spread * jax.random.normal(stream_key, extent, jnp.float32)
    if cuts:
        values = values * level_of(stream_key, extent, cuts, -0.22, 0.18)
    return jnp.clip(strengthened(values, jax.random.fold_in(stream_key, 3), *heavy), -reach, reach).astype(held_as)


def setup_inputs(seed: int = 0) -> dict:
    key_of = jax.random.split(jax.random.key(seed), 7)
    return {
        "front_slab": heavy_noise(key_of[0], (M, N), N ** -0.5, 0.046875, ((0, 4), (1, 64)), (1, 0, 64, 4.0)),
        "omega_codes": touch_ends(jax.random.randint(key_of[1], (N, R), -3, 4), jax.random.fold_in(key_of[1], 1), -3, 3).astype(jnp.int32),
        "block_mask": touch_ends((jax.random.randint(key_of[2], (MB, NB), 0, 4) < 3).astype(jnp.int32), jax.random.fold_in(key_of[2], 1), 0, 1),
        "leaf_pivots": draw_leaf_pivots(jax.random.fold_in(key_of[6], 71), 0),
        "mid_pivots": draw_mid_pivots(jax.random.fold_in(key_of[6], 71), 0),
        "root_pivots": draw_root_pivots(jax.random.fold_in(key_of[6], 71), 0),
    }


def interpolate(sample_block, skeleton):
    gram_matrix = jnp.dot(skeleton.astype(jnp.float32), skeleton.T.astype(jnp.float32), precision=lax.Precision.HIGHEST, preferred_element_type=jnp.float32)
    factor = jnp.linalg.cholesky(gram_matrix)
    cross_terms = jnp.dot(skeleton.astype(jnp.float32), sample_block.T.astype(jnp.float32), precision=lax.Precision.HIGHEST, preferred_element_type=jnp.float32)
    return jax.scipy.linalg.cho_solve((factor, True), cross_terms).T

def reference(front_slab, omega_codes, block_mask, leaf_pivots, mid_pivots, root_pivots):
    sketch = omega_codes.astype(jnp.bfloat16) * jnp.bfloat16(0.5)
    columns = jnp.arange(N, dtype=jnp.int32)
    region = jnp.where(columns < M, columns // MS, NODES).astype(jnp.int32)

    def subtree_work(subtree):
        slab_rows = lax.dynamic_slice_in_dim(front_slab, subtree * MS, MS, 0)
        marks = lax.dynamic_slice_in_dim(block_mask, subtree * (MS // BR), MS // BR, 0)
        masked = (slab_rows.reshape(MS // BR, BR, NB, BC) * marks.astype(jnp.bfloat16)[:, None, :, None]).reshape(MS, N)
        off_range = (region != subtree).astype(jnp.bfloat16)
        samples = jnp.dot(masked.astype(jnp.float32), (sketch * off_range[:, None]).astype(jnp.float32), preferred_element_type=jnp.float32)
        picked = jnp.take(masked, leaf_pivots[subtree].astype(jnp.int32), axis=0)
        range_parts = []
        for segment in range(NODES):
            range_parts.append(jnp.dot(picked[:, segment * MS:(segment + 1) * MS].astype(jnp.float32), sketch[segment * MS:(segment + 1) * MS].astype(jnp.float32), preferred_element_type=jnp.float32))
        range_parts.append(jnp.dot(picked[:, M:].astype(jnp.float32), sketch[M:].astype(jnp.float32), preferred_element_type=jnp.float32))
        return (samples, jnp.stack(range_parts, axis=1))
    samples, pieces = lax.map(subtree_work, jnp.arange(NODES, dtype=jnp.int32))
    groups = jnp.arange(NODES + 1, dtype=jnp.int32)
    leaf_parts = []
    outer_list = []
    far_list = []
    for subtree in range(NODES):
        leaf_sel = (groups != subtree).astype(jnp.float32)
        outer_sel = (groups // 2 != subtree // 2).astype(jnp.float32)
        leaf_skeleton = jnp.einsum('kjs,j->ks', pieces[subtree], leaf_sel, precision=lax.Precision.HIGHEST)
        leaf_parts.append(interpolate(samples[subtree], leaf_skeleton))
        outer_list.append(jnp.einsum('kjs,j->ks', pieces[subtree], outer_sel, precision=lax.Precision.HIGHEST))
        far_list.append(pieces[subtree][:, NODES, :])
    leaf_interp = jnp.concatenate(leaf_parts, axis=0)
    mid_parts = []
    upper_list = []
    for parent in range(2):
        stack = jnp.concatenate([outer_list[2 * parent], outer_list[2 * parent + 1]], axis=0)
        chosen = mid_pivots[parent].astype(jnp.int32)
        mid_skeleton = jnp.take(stack, chosen, axis=0)
        mid_parts.append(interpolate(stack, mid_skeleton))
        far_stack = jnp.concatenate([far_list[2 * parent], far_list[2 * parent + 1]], axis=0)
        upper_list.append(jnp.take(far_stack, chosen, axis=0))
    mid_interp = jnp.concatenate(mid_parts, axis=0)
    top_rows = jnp.concatenate(upper_list, axis=0)
    root_skeleton = jnp.take(top_rows, root_pivots.astype(jnp.int32), axis=0)
    root_interp = interpolate(top_rows, root_skeleton)
    return (leaf_interp, mid_interp, root_interp, root_skeleton)
```

```python
import jax
import jax.numpy as jnp
from jax import lax
from jax.experimental import pallas as pl
from jax.experimental.pallas import tpu as pltpu
from jax.sharding import PartitionSpec as P

F32 = jnp.float32
BF16 = jnp.bfloat16
MESH = pl.DeviceIdType.MESH
TOP = lax.Precision.HIGHEST

NX, NY, NZ, NC = 4, 4, 8, 2
SIDE = 128
SAMPLES = 384
CHUNK = 256
HALF = SAMPLES // NC
PART = HALF // NY


def exact_dot(a, b):
    return jnp.dot(a, b, precision=TOP, preferred_element_type=F32)


def flip(block):
    rows, cols = block.shape
    return jnp.concatenate(
        [
            jnp.concatenate(
                [block[i : i + SIDE, j : j + SIDE].T for i in range(0, rows, SIDE)], axis=1
            )
            for j in range(0, cols, SIDE)
        ],
        axis=0,
    )


def inverses(matrices):
    n, b = SIDE, 8
    lane = lax.broadcasted_iota(jnp.int32, (8, n), 1)
    sub = lax.broadcasted_iota(jnp.int32, (8, n), 0)
    work = [[m[8 * g : 8 * g + 8, :] for g in range(n // 8)] for m in matrices]
    for k in range(0, n, b):
        own = k // 8
        inside = (lane >= k) & (lane < k + b)
        for t, m in enumerate(work):
            col = [
                [jnp.broadcast_to(m[g][:, k + j : k + j + 1], (8, n)) for g in range(n // 8)]
                for j in range(b)
            ]
            row = [jnp.broadcast_to(m[own][j : j + 1, :], (8, n)) for j in range(b)]
            e = [[None] * b for _ in range(b)]
            for i in range(b):
                for j in range(i, b):
                    e[i][j] = jnp.broadcast_to(col[j][own][i : i + 1, :], (8, n))
            u = [jnp.where(inside, jnp.where(lane == k + j, -1.0, 0.0), row[j]) for j in range(b)]
            d = [None] * b
            low = [[None] * b for _ in range(b)]
            for j in range(b):
                d[j] = pltpu.reciprocal(e[j][j], approx=False)
                for i in range(j + 1, b):
                    low[i][j] = e[j][i] * d[j]
                    for q in range(i, b):
                        e[i][q] = e[i][q] - low[i][j] * e[j][q]
                    u[i] = u[i] - low[i][j] * u[j]
            v = [None] * b
            for i in reversed(range(b)):
                v[i] = d[i] * u[i]
                for q in range(i + 1, b):
                    v[i] = v[i] - low[q][i] * v[q]
            new = []
            for g in range(n // 8):
                z = jnp.where(inside, 0.0, m[g])
                if g == own:
                    z = jnp.zeros_like(z)
                for j in range(b):
                    c = col[j][g]
                    if g == own:
                        c = jnp.where(sub == j, -1.0, 0.0)
                    z = z - c * v[j]
                new.append(z)
            work[t] = new
    return [-jnp.concatenate(m, axis=0) for m in work]


def kernel(
    slab_hbm, codes_hbm, marks, leaf_piv, mid_piv, root_piv,
    leaf_out, mid_out, root_out, skel_out,
    slab, codes, omega, tall, tall_in, qt, cb, hb, yb, zb, rz, rzo, fo, st,
    xf, xo, mt, xh, xyb, xz, xzb,
    load_sem, send_sem, recv_sem,
):
    n = lax.axis_index("node")
    r = lax.axis_index("row")
    y, z, c = r // (NZ * NC), (r // NC) % NZ, r % NC
    chunks = slab.shape[0] // CHUNK
    width = slab.shape[1]
    span = slab.shape[0]
    mark_width = width // marks.shape[1]

    def where_is(x_at, y_at, z_at, c_at):
        return (x_at, y_at * (NZ * NC) + z_at * NC + c_at)

    load_omega = pltpu.make_async_copy(codes_hbm, codes, load_sem.at[chunks])
    load_omega.start()
    loads = []
    for a in range(chunks):
        place = pl.ds(a * CHUNK, CHUNK)
        loads.append(
            pltpu.make_async_copy(slab_hbm.at[place], slab.at[place], load_sem.at[a])
        )
        loads[-1].start()

    sibling = where_is(n, y, z, 1 - c)
    on_y = [where_is(n, (y + d) % NY, z, c) for d in range(1, NY)]
    on_z = [where_is(n, y, (z + d) % NZ, c) for d in range(1, NZ)]
    on_x = [where_is((n + d) % NX, y, z, c) for d in range(1, NX)]
    pair = where_is(n + 1 - 2 * (n % 2), y, z, c)
    barrier = pltpu.get_barrier_semaphore()
    friends = [sibling] + on_y + on_z + on_x
    for friend in friends:
        pl.semaphore_signal(barrier, inc=1, device_id=friend, device_id_type=MESH)

    count = [0]
    sent = []

    def remote(src, dst, to):
        at = count[0]
        count[0] += 1
        return pltpu.make_async_remote_copy(
            src_ref=src, dst_ref=dst, send_sem=send_sem.at[at], recv_sem=recv_sem.at[at],
            device_id=to, device_id_type=MESH,
        )

    def go(copy):
        copy.start()
        sent.append(copy)

    lane = lax.broadcasted_iota(jnp.int32, (1, width), 1)
    column = lane + r * width
    region = jnp.where(column < NX * span, column // span, NX)
    off_leaf = (region != n).astype(F32)
    off_outer = (region // 2 != n // 2).astype(F32)
    off_far = (region == NX).astype(F32)
    mark_of = lane // mark_width

    def masked(a):
        keep = jnp.zeros_like(off_leaf)
        for b in range(marks.shape[1]):
            keep = jnp.where(mark_of == b, marks[a, b].astype(F32), keep)
        keep = (keep * off_leaf).astype(BF16)
        return slab[pl.ds(pl.multiple_of(a * CHUNK, CHUNK), CHUNK), :] * keep

    load_omega.wait()
    omega[...] = (codes[...].astype(F32) * 0.5).astype(BF16)
    piv_rows = jnp.broadcast_to(leaf_piv[0:1, :].astype(F32), (SIDE, SIDE)).T.astype(jnp.int32)
    spot = lax.broadcasted_iota(jnp.int32, (SIDE, SIDE), 1)
    picked = jnp.zeros((SIDE, width), F32)
    for a in range(chunks):
        loads[a].wait()
        pick = jnp.concatenate(
            [
                jnp.where(piv_rows == spot + (a * CHUNK + h), 1.0, 0.0)
                for h in range(0, CHUNK, SIDE)
            ],
            axis=1,
        ).astype(BF16)
        picked = picked + jnp.dot(pick, masked(a), preferred_element_type=F32)

    special = z <= 2
    near = special & (y == 0)
    part_l = flip(jnp.dot(picked.astype(BF16), omega[...], preferred_element_type=F32))
    qt[0] = part_l

    @pl.when(special & (y != 0))
    def _():
        qt[1] = part_l
        qt[2] = part_l

    @pl.when(near)
    def _():
        for i, off in ((1, off_outer), (2, off_far)):
            part = jnp.dot((picked * off).astype(BF16), omega[...], preferred_element_type=F32)
            qt[i] = flip(part)

    pl.semaphore_wait(barrier, len(friends))

    away = pl.ds((1 - c) * HALF, HALF)
    mine = pl.ds(c * HALF, HALF)
    c_l = remote(qt.at[0, away], cb.at[0], sibling)
    c_of = remote(qt.at[pl.ds(1, 2), away], cb.at[pl.ds(1, 2)], sibling)
    go(c_l)
    pl.when(special)(c_of.start)

    def tall_chunk(a):
        res = jnp.dot(masked(a), omega[...], preferred_element_type=F32)
        at_y, z0 = a // 2, (a % 2) * (CHUNK // 64)
        for i in range(CHUNK // 32):
            zz, cc = i // 2, i % 2
            rows = pl.ds(pl.multiple_of((z0 + zz) * 32, 32), 32)
            tall[cc, at_y, rows, :] = res[i * 32 : (i + 1) * 32]

    tall_copies = [remote(tall.at[1 - c, q], tall_in.at[q], sibling) for q in range(NY)]

    def tall_part(q):
        tall_chunk(2 * q)
        tall_chunk(2 * q + 1)
        go(tall_copies[q])

    tall_part(0)
    c_l.wait_recv()
    hb[0] = qt[0, mine, :] + cb[0]
    y_l = [remote(hb.at[0, pl.ds((y + d) % NY * PART, PART)], yb.at[d - 1, 0], on_y[d - 1]) for d in range(1, NY)]
    y_of = [
        remote(hb.at[pl.ds(1, 2), pl.ds((y + d) % NY * PART, PART)], yb.at[d - 1, pl.ds(1, 2)], on_y[d - 1])
        for d in range(1, NY)
    ]
    for d in (2, 1, 3):
        go(y_l[d - 1])

    @pl.when(special)
    def _():
        c_of.wait_recv()
        for i in (1, 2):
            hb[i] = qt[i, mine, :] + cb[i]
        for d in (2, 1, 3):
            y_of[d - 1].start()

    for q in range(1, NY):
        tall_part(q)

    own_y = pl.ds(y * PART, PART)
    for d in range(1, NY):
        y_l[d - 1].wait_recv()
    zb[0] = hb[0, own_y, :] + yb[0, 0] + yb[1, 0] + yb[2, 0]
    z_order = (4, 3, 5, 2, 6, 1, 7)
    z_l = [remote(zb.at[0], rz.at[z], on_z[d - 1]) for d in range(1, NZ)]
    z_of = [remote(zb.at[pl.ds(1, 2)], rzo.at[z], on_z[d - 1]) for d in range(1, NZ)]
    for d in z_order:
        go(z_l[d - 1])
    rz[z] = zb[0]

    @pl.when(special)
    def _():
        for d in range(1, NY):
            y_of[d - 1].wait_recv()
        for i in (1, 2):
            zb[i] = hb[i, own_y, :] + yb[0, i] + yb[1, i] + yb[2, i]
        for d in z_order:
            z_of[d - 1].start()
        rzo[z] = zb[1:3]

    for q in range(NY):
        tall_copies[q].wait_recv()
        tall_in[q] = tall_in[q] + tall[c, q]

    for d in range(1, NZ):
        z_l[d - 1].wait_recv()
    total = rz[0]
    for i in range(1, NZ):
        total = total + rz[i]
    here = c * HALF + y * PART
    st[pl.ds(here, PART), :] = total

    def spread(ref_at, sends_y):
        pass

    def st_at(y_at):
        return st.at[pl.ds(c * HALF + y_at * PART, PART)]

    s_y = [remote(st_at(y), st_at(y), on_y[d - 1]) for d in range(1, NY)]
    s_c = [remote(st_at((y + NY - d) % NY), st_at((y + NY - d) % NY), sibling) for d in range(NY)]
    for d in (2, 1, 3):
        go(s_y[d - 1])
    go(s_c[0])

    for i in range(NZ):
        is_special = i <= 2
        if is_special:

            @pl.when(z != i)
            def _():
                for d in range(1, NZ):

                    @pl.when((z + NZ - d) % NZ == i)
                    def _():
                        z_of[d - 1].wait_recv()

    for i in range(2):
        part = rzo[0, i] + rzo[1, i] + rzo[2, i]
        for j in range(3, NZ):
            part = part + rz[j]
        fo[i] = part
    xo[n % 2] = fo[0]
    xf[n] = fo[1]
    x_o = remote(fo.at[0], xo.at[n % 2], pair)
    x_f = [remote(fo.at[1], xf.at[n], on_x[d - 1]) for d in range(1, NX)]
    go(x_f[1])
    go(x_o)
    go(x_f[0])
    go(x_f[2])

    for d in range(1, NY):
        s_y[d - 1].wait_recv()
        go(s_c[d])

    x_o.wait_recv()
    for d in range(1, NX):
        x_f[d - 1].wait_recv()
    from_sub = lax.broadcasted_iota(jnp.int32, (2 * SIDE, SIDE), 0)

    def chooser(row):
        return jnp.where(from_sub == row, 1.0, 0.0)

    parent = n // 2
    choose_mid = [chooser(mid_piv[q : q + 1, :]) for q in range(2)]
    choose_own = jnp.where(parent == 0, choose_mid[0], choose_mid[1])
    upper = [
        exact_dot(jnp.concatenate([xf[2 * q], xf[2 * q + 1]], axis=1), choose_mid[q])
        for q in range(2)
    ]
    own_part = pl.ds(here, PART)
    mt[0, own_part, :] = exact_dot(jnp.concatenate([xo[0], xo[1]], axis=1), choose_own)
    mt[1, own_part, :] = fo[0]
    mt[2, own_part, :] = exact_dot(jnp.concatenate(upper, axis=1), chooser(root_piv[0:1, :]))
    mt[3, own_part, :] = jnp.where(parent == 0, upper[0], upper[1])

    def mt_at(y_at):
        return mt.at[:, pl.ds(c * HALF + y_at * PART, PART)]

    m_y = [remote(mt_at(y), mt_at(y), on_y[d - 1]) for d in range(1, NY)]
    m_c = [remote(mt_at((y + NY - d) % NY), mt_at((y + NY - d) % NY), sibling) for d in range(NY)]
    for d in (2, 1, 3):
        go(m_y[d - 1])
    go(m_c[0])

    for copy in s_c:
        copy.wait_recv()
    skeleton_t = st[...]
    for q in range(NY):
        xh[q] = exact_dot(tall_in[q], skeleton_t)
    l_y = [remote(xh.at[(y + d) % NY], xyb.at[d - 1], on_y[d - 1]) for d in range(1, NY)]
    for d in (2, 1, 3):
        go(l_y[d - 1])

    leaf_inv = inverses([exact_dot(flip(skeleton_t), skeleton_t)])[0]

    for d in range(1, NY):
        m_y[d - 1].wait_recv()
        go(m_c[d])
    for copy in l_y:
        copy.wait_recv()
    xz[...] = xh[y] + xyb[0] + xyb[1] + xyb[2]
    l_z = [remote(xz.at[pl.ds((z + d) % NZ * 32, 32)], xzb.at[d - 1], on_z[d - 1]) for d in range(1, NZ)]
    for d in z_order:
        go(l_z[d - 1])

    for copy in m_c:
        copy.wait_recv()
    mid_t, outer_t, root_t, top_t = (mt[i] for i in range(4))
    root_skeleton = flip(root_t)
    skel_out[...] = root_skeleton
    mid_inv, root_inv = inverses([exact_dot(flip(mid_t), mid_t), exact_dot(root_skeleton, root_t)])
    mid_out[...] = exact_dot(exact_dot(flip(outer_t), mid_t), mid_inv)
    top_all = exact_dot(exact_dot(flip(top_t), root_t), root_inv)
    root_out[...] = jnp.where(n % 2 == 0, top_all[: SIDE // 2], top_all[SIDE // 2 :])

    cross = xz[pl.ds(z * 32, 32), :]
    for d in range(1, NZ):
        l_z[d - 1].wait_recv()
        cross = cross + xzb[d - 1]
    leaf_out[...] = exact_dot(cross, leaf_inv)

    for copy in sent:
        copy.wait_send()

    @pl.when(special)
    def _():
        c_of.wait_send()
        for copy in y_of + z_of:
            copy.wait_send()


COPIES = 80


def per_device(front_slab, omega_codes, block_mask, leaf_pivots, mid_pivots, root_pivots):
    height, width = front_slab.shape
    samples = omega_codes.shape[1]
    vmem = pl.BlockSpec(memory_space=pltpu.VMEM)
    anywhere = pl.BlockSpec(memory_space=pl.ANY)
    share = height // (NY * NZ * NC)
    half = height // NC
    return pl.pallas_call(
        kernel,
        out_shape=(
            jax.ShapeDtypeStruct((share, SIDE), F32),
            jax.ShapeDtypeStruct((SIDE, SIDE), F32),
            jax.ShapeDtypeStruct((SIDE // 2, SIDE), F32),
            jax.ShapeDtypeStruct((SIDE, samples), F32),
        ),
        in_specs=[anywhere, anywhere, pl.BlockSpec(memory_space=pltpu.SMEM), vmem, vmem, vmem],
        out_specs=(vmem,) * 4,
        scratch_shapes=[
            pltpu.VMEM((height, width), BF16),
            pltpu.VMEM((width, samples), jnp.int32),
            pltpu.VMEM((width, samples), BF16),
            pltpu.VMEM((NC, NY, half // NY, samples), F32),
            pltpu.VMEM((NY, half // NY, samples), F32),
            pltpu.VMEM((3, samples, SIDE), F32),
            pltpu.VMEM((3, HALF, SIDE), F32),
            pltpu.VMEM((3, HALF, SIDE), F32),
            pltpu.VMEM((NY - 1, 3, PART, SIDE), F32),
            pltpu.VMEM((3, PART, SIDE), F32),
            pltpu.VMEM((NZ, PART, SIDE), F32),
            pltpu.VMEM((NZ, 2, PART, SIDE), F32),
            pltpu.VMEM((2, PART, SIDE), F32),
            pltpu.VMEM((samples, SIDE), F32),
            pltpu.VMEM((NX, PART, SIDE), F32),
            pltpu.VMEM((2, PART, SIDE), F32),
            pltpu.VMEM((4, samples, SIDE), F32),
            pltpu.VMEM((NY, half // NY, SIDE), F32),
            pltpu.VMEM((NY - 1, half // NY, SIDE), F32),
            pltpu.VMEM((half // NY, SIDE), F32),
            pltpu.VMEM((NZ - 1, share, SIDE), F32),
            pltpu.SemaphoreType.DMA((16,)),
            pltpu.SemaphoreType.DMA((COPIES,)),
            pltpu.SemaphoreType.DMA((COPIES,)),
        ],
        compiler_params=pltpu.CompilerParams(
            collective_id=0, has_side_effects=True, vmem_limit_bytes=56 << 20
        ),
    )(front_slab, omega_codes, block_mask, leaf_pivots, mid_pivots, root_pivots.reshape(1, SIDE))


def solution(mesh):
    return jax.shard_map(
        per_device,
        mesh=mesh,
        in_specs=(P("node", "row"), P("row", None), P("node", "row"), P("node", None), P(), P()),
        out_specs=(P(("node", "row"), None), P("node", None), P("node", None), P()),
        check_vma=False,
    )
```

```python
import jax
import jax.numpy as jnp
from jax import lax
from jax.experimental import pallas as pl
from jax.experimental.pallas import tpu as pltpu
from jax.sharding import PartitionSpec as P

F32 = jnp.float32
BF16 = jnp.bfloat16
MESH = pl.DeviceIdType.MESH
TOP = lax.Precision.HIGHEST

NX, NY, NZ, NC = 4, 4, 8, 2
SIDE = 128
SAMPLES = 384
CHUNK = 256
HALF = SAMPLES // NC
PART = HALF // NY
SPLIT = 48
PIECE = 16


def exact_dot(a, b):
    return jnp.dot(a, b, precision=TOP, preferred_element_type=F32)


def choose_dot(a, chosen):
    high = a.astype(BF16)
    rest = a - high.astype(F32)
    middle = rest.astype(BF16)
    low = (rest - middle.astype(F32)).astype(BF16)
    return sum(jnp.dot(t, chosen, preferred_element_type=F32) for t in (low, middle, high))


def flip(block):
    rows, cols = block.shape
    return jnp.concatenate(
        [
            jnp.concatenate(
                [block[i : i + SIDE, j : j + SIDE].T for i in range(0, rows, SIDE)], axis=1
            )
            for j in range(0, cols, SIDE)
        ],
        axis=0,
    )


def pivot_rows(rows, k):
    b, n = 8, SIDE
    lane = lax.broadcasted_iota(jnp.int32, (b, n), 1)
    inside = (lane >= k) & (lane < k + b)
    col = [jnp.broadcast_to(rows[:, k + j : k + j + 1], (b, n)) for j in range(b)]
    e = [[None] * b for _ in range(b)]
    for i in range(b):
        for j in range(i, b):
            e[i][j] = jnp.broadcast_to(col[j][i : i + 1, :], (b, n))
    u = [
        jnp.where(
            inside,
            jnp.where(lane == k + j, -1.0, 0.0),
            jnp.broadcast_to(rows[j : j + 1, :], (b, n)),
        )
        for j in range(b)
    ]
    d = [None] * b
    low = [[None] * b for _ in range(b)]
    for j in range(b):
        d[j] = pltpu.reciprocal(e[j][j], approx=False)
        for i in range(j + 1, b):
            low[i][j] = e[j][i] * d[j]
            for q in range(i, b):
                e[i][q] = e[i][q] - low[i][j] * e[j][q]
            u[i] = u[i] - low[i][j] * u[j]
    v = [None] * b
    for i in reversed(range(b)):
        v[i] = d[i] * u[i]
        for q in range(i + 1, b):
            v[i] = v[i] - low[q][i] * v[q]
    return v


def row_groups(matrix):
    return [matrix[8 * g : 8 * g + 8, :] for g in range(SIDE // 8)]


def swept(work):
    return [-jnp.concatenate(m, axis=0) for m in work]


def sweep(work, first, last, by_dot):
    b, n = 8, SIDE
    groups = n // b
    lane = lax.broadcasted_iota(jnp.int32, (b, n), 1)
    sub = lax.broadcasted_iota(jnp.int32, (b, n), 0)
    work = list(work)
    for k in range(first, last, b):
        own = k // b
        inside = (lane >= k) & (lane < k + b)
        pivots = [pivot_rows(m[own], k) for m in work]
        for t, m in enumerate(work):
            v = pivots[t]
            new = [None] * groups
            new[own] = v[0]
            for j in range(1, b):
                new[own] = jnp.where(sub == j, v[j], new[own])
            order = [(own + 1 + q) % groups for q in range(groups - 1)]
            if by_dot:
                update = exact_dot(jnp.concatenate(m, axis=0)[:, k : k + b], new[own])
            for at, g in enumerate(order):
                part = jnp.where(inside, 0.0, m[g])
                if by_dot and at > 0:
                    part = part - update[b * g : b * g + b]
                else:
                    for j in range(b):
                        part = part - jnp.broadcast_to(m[g][:, k + j : k + j + 1], (b, n)) * v[j]
                new[g] = part
            work[t] = new
    return work


def kernel(
    slab_hbm, codes_hbm, marks, leaf_piv, mid_piv, root_piv,
    leaf_out, mid_out, root_out, skel_out,
    slab, codes, omega, tall, tall_in, qt, cb, hb, yb, zb, rz, rzo, fo, st,
    xf, xo, mo, mt, xh, x1_in, x2_in, x1, x2, y1_in, y2_in, kept,
    load_sem, send_sem, recv_sem,
):
    n = lax.axis_index("node")
    r = lax.axis_index("row")
    y, z, c = r // (NZ * NC), (r // NC) % NZ, r % NC
    chunks = slab.shape[0] // CHUNK
    width = slab.shape[1]
    span = slab.shape[0]
    mark_width = width // marks.shape[0]

    def where_is(x_at, y_at, z_at, c_at):
        return (x_at, y_at * (NZ * NC) + z_at * NC + c_at)

    def apart(work):
        pl.when(r >= 0)(work)

    load_omega = pltpu.make_async_copy(codes_hbm, codes, load_sem.at[chunks])
    load_omega.start()
    loads = []
    for a in range(chunks):
        place = pl.ds(a * CHUNK, CHUNK)
        loads.append(
            pltpu.make_async_copy(slab_hbm.at[place], slab.at[place], load_sem.at[a])
        )
        loads[-1].start()

    sibling = where_is(n, y, z, 1 - c)
    on_y = [where_is(n, (y + d) % NY, z, c) for d in range(1, NY)]
    on_z = [where_is(n, y, (z + d) % NZ, c) for d in range(1, NZ)]
    on_x = [where_is((n + d) % NX, y, z, c) for d in range(1, NX)]
    pair = where_is(n + 1 - 2 * (n % 2), y, z, c)
    barrier = pltpu.get_barrier_semaphore()
    friends = [sibling] + on_y + on_z + on_x
    for friend in friends:
        pl.semaphore_signal(barrier, inc=1, device_id=friend, device_id_type=MESH)

    count = [0]
    sent = []

    def remote(src, dst, to):
        at = count[0]
        count[0] += 1
        return pltpu.make_async_remote_copy(
            src_ref=src, dst_ref=dst, send_sem=send_sem.at[at], recv_sem=recv_sem.at[at],
            device_id=to, device_id_type=MESH,
        )

    def go(copy):
        copy.start()
        sent.append(copy)

    lane = lax.broadcasted_iota(jnp.int32, (1, width), 1)
    column = lane + r * width
    region = jnp.where(column < NX * span, column // span, NX)
    off_leaf = (region != n).astype(F32)
    off_outer = (region // 2 != n // 2).astype(F32)
    off_far = (region == NX).astype(F32)
    mark_of = lane // mark_width

    def masked(a):
        keep = jnp.zeros_like(off_leaf)
        for b in range(marks.shape[0]):
            keep = jnp.where(mark_of == b, marks[b, a].astype(F32), keep)
        keep = (keep * off_leaf).astype(BF16)
        return slab[pl.ds(pl.multiple_of(a * CHUNK, CHUNK), CHUNK), :] * keep

    load_omega.wait()
    omega[...] = (codes[...].astype(F32) * 0.5).astype(BF16)
    piv_rows = jnp.broadcast_to(leaf_piv[0:1, :].astype(F32), (SIDE, SIDE)).T.astype(jnp.int32)
    spot = lax.broadcasted_iota(jnp.int32, (SIDE, SIDE), 1)
    picked = jnp.zeros((SIDE, width), F32)
    for a in range(chunks):
        loads[a].wait()
        pick = jnp.concatenate(
            [
                jnp.where(piv_rows == spot + (a * CHUNK + h), 1.0, 0.0)
                for h in range(0, CHUNK, SIDE)
            ],
            axis=1,
        ).astype(BF16)
        picked = picked + jnp.dot(pick, masked(a), preferred_element_type=F32)

    special = z <= 2
    near = special & (y == 0)
    qt[0] = flip(jnp.dot(picked.astype(BF16), omega[...], preferred_element_type=F32))
    pl.semaphore_wait(barrier, len(friends))

    away = pl.ds((1 - c) * HALF, HALF)
    mine = pl.ds(c * HALF, HALF)
    c_l = remote(qt.at[0, away], cb.at[0], sibling)
    c_of = remote(qt.at[pl.ds(1, 2), away], cb.at[pl.ds(1, 2)], sibling)
    go(c_l)

    @pl.when(near)
    def _():
        for i, off in ((1, off_outer), (2, off_far)):
            part = jnp.dot((picked * off).astype(BF16), omega[...], preferred_element_type=F32)
            qt[i] = flip(part)
        c_of.start()

    def tall_chunk(a):
        res = jnp.dot(masked(a), omega[...], preferred_element_type=F32)
        at_y, z0 = a // 2, (a % 2) * (CHUNK // 64)
        for i in range(CHUNK // 32):
            zz, cc = i // 2, i % 2
            rows = pl.ds(pl.multiple_of((z0 + zz) * 32, 32), 32)
            tall[cc, at_y, rows, :] = res[i * 32 : (i + 1) * 32]

    tall_copies = [remote(tall.at[1 - c, q], tall_in.at[q], sibling) for q in range(NY)]

    def tall_part(q):
        @apart
        def _():
            tall_chunk(2 * q)
            tall_chunk(2 * q + 1)

        go(tall_copies[q])

    tall_part(0)
    c_l.wait_recv()
    hb[0] = qt[0, mine, :] + cb[0]
    y_l = [remote(hb.at[0, pl.ds((y + d) % NY * PART, PART)], yb.at[d - 1, 0], on_y[d - 1]) for d in range(1, NY)]
    y_of = [
        remote(hb.at[pl.ds(1, 2), pl.ds((y + d) % NY * PART, PART)], yb.at[d - 1, pl.ds(1, 2)], on_y[d - 1])
        for d in range(1, NY)
    ]
    for d in (2, 1, 3):
        go(y_l[d - 1])

    @pl.when(near)
    def _():
        c_of.wait_recv()
        for i in (1, 2):
            hb[i] = qt[i, mine, :] + cb[i]
        for d in (2, 1, 3):
            y_of[d - 1].start()

    tall_part(1)

    own_y = pl.ds(y * PART, PART)
    for d in range(1, NY):
        y_l[d - 1].wait_recv()
    zb[0] = hb[0, own_y, :] + yb[0, 0] + yb[1, 0] + yb[2, 0]
    z_order = (4, 3, 5, 2, 6, 1, 7)
    z_l = [remote(zb.at[0], rz.at[z], on_z[d - 1]) for d in range(1, NZ)]
    z_of = [remote(zb.at[pl.ds(1, 2)], rzo.at[z], on_z[d - 1]) for d in range(1, NZ)]
    for d in z_order:
        go(z_l[d - 1])
    rz[z] = zb[0]

    @pl.when(near)
    def _():
        for i in (1, 2):
            zb[i] = hb[i, own_y, :] + yb[0, 0] + yb[1, 0] + yb[2, 0]

    for d in range(1, NY):

        @pl.when(special & (y == d))
        def _():
            y_of[d - 1].wait_recv()
            base = hb[0, own_y, :]
            for other in range(1, NY):
                if other != d:
                    base = base + yb[other - 1, 0]
            for i in (1, 2):
                zb[i] = base + yb[d - 1, i]

    @pl.when(special)
    def _():
        for d in z_order:
            z_of[d - 1].start()
        rzo[z] = zb[1:3]

    tall_part(2)
    tall_part(3)

    for d in range(1, NZ):
        z_l[d - 1].wait_recv()
    total = rz[0]
    for i in range(1, NZ):
        total = total + rz[i]
    here = c * HALF + y * PART
    st[pl.ds(here, PART), :] = total

    def rows_of(y_at):
        return pl.ds(c * HALF + y_at * PART, PART)

    def gather(view):
        along = [remote(view(y), view(y), on_y[d - 1]) for d in range(1, NY)]
        across = [remote(view((y + NY - d) % NY), view((y + NY - d) % NY), sibling) for d in range(NY)]
        return along, across

    def begin(along, across):
        for d in (2, 1, 3):
            go(along[d - 1])
        go(across[0])

    def forward(along, across):
        for d in range(1, NY):
            along[d - 1].wait_recv()
            go(across[d])

    s_y, s_c = gather(lambda y_at: st.at[rows_of(y_at)])
    begin(s_y, s_c)

    for q in range(NY):
        tall_copies[q].wait_recv()
        tall_in[q] = tall_in[q] + tall[c, q]

    forward(s_y, s_c)
    for copy in s_c:
        copy.wait_recv()
    skeleton_t = st[...]
    first_y = [remote(xh.at[0, (y + d) % NY], x1_in.at[d - 1], on_y[d - 1]) for d in range(1, NY)]
    first_z = [remote(xh.at[1, :, (z + d) % NZ], x2_in.at[d - 1], on_z[d - 1]) for d in range(1, NZ)]
    for d in (2, 1, 3, 0):
        at_y = (y + d) % NY
        cross = exact_dot(tall_in[at_y], skeleton_t)
        for i in range(NZ * 2):
            xh[i % 2, at_y, i // 2] = cross[i * PIECE : (i + 1) * PIECE]
        if d:
            go(first_y[d - 1])

    for i in range(3):

        @pl.when(z != i)
        def _():
            for d in range(1, NZ):

                @pl.when((z + NZ - d) % NZ == i)
                def _():
                    z_of[d - 1].wait_recv()

    for i in range(2):
        part = rzo[0, i] + rzo[1, i] + rzo[2, i]
        for j in range(3, NZ):
            part = part + rz[j]
        fo[i] = part
    xo[n % 2] = fo[0]
    xf[n] = fo[1]
    x_o = remote(fo.at[0], xo.at[n % 2], pair)
    x_f = [remote(fo.at[1], xf.at[n], on_x[d - 1]) for d in range(1, NX)]
    go(x_f[1])
    go(x_o)
    go(x_f[0])
    go(x_f[2])
    for d in z_order:
        go(first_z[d - 1])
    own_part = pl.ds(here, PART)
    mo[own_part, :] = fo[0]
    o_y, o_c = gather(lambda y_at: mo.at[rows_of(y_at)])
    begin(o_y, o_c)

    from_sub = lax.broadcasted_iota(jnp.int32, (2 * SIDE, SIDE), 0)

    def chooser(row):
        return jnp.where(from_sub == row, 1.0, 0.0).astype(BF16)

    parent = n // 2
    choose_mid = [chooser(mid_piv[q : q + 1, :]) for q in range(2)]
    choose_own = jnp.where(parent == 0, choose_mid[0], choose_mid[1])
    @apart
    def _():
        work = [row_groups(exact_dot(flip(st[...]), st[...]))]
        kept[...] = jnp.concatenate(sweep(work, 0, SPLIT, False)[0], axis=0)

    x_o.wait_recv()
    for d in range(1, NX):
        x_f[d - 1].wait_recv()
    upper = [
        choose_dot(jnp.concatenate([xf[2 * q], xf[2 * q + 1]], axis=1), choose_mid[q])
        for q in range(2)
    ]
    mt[0, own_part, :] = choose_dot(jnp.concatenate([xo[0], xo[1]], axis=1), choose_own)
    mt[1, own_part, :] = choose_dot(jnp.concatenate(upper, axis=1), chooser(root_piv[0:1, :]))
    mt[2, own_part, :] = jnp.where(parent == 0, upper[0], upper[1])
    m_y, m_c = gather(lambda y_at: mt.at[:, rows_of(y_at)])
    begin(m_y, m_c)
    forward(o_y, o_c)

    @apart
    def _():
        kept[...] = swept(sweep([row_groups(kept[...])], SPLIT, SIDE, False))[0]


    for copy in first_y:
        copy.wait_recv()
    x1[...] = xh[0, y] + x1_in[0] + x1_in[1] + x1_in[2]
    then_z = [remote(x1.at[(z + d) % NZ], y1_in.at[d - 1], on_z[d - 1]) for d in range(1, NZ)]
    for d in z_order:
        go(then_z[d - 1])

    forward(m_y, m_c)
    for copy in first_z:
        copy.wait_recv()
    total2 = xh[1, :, z]
    for d in range(1, NZ):
        total2 = total2 + x2_in[d - 1]
    x2[...] = total2
    then_y = [remote(x2.at[(y + d) % NY], y2_in.at[d - 1], on_y[d - 1]) for d in range(1, NY)]
    for d in (2, 1, 3):
        go(then_y[d - 1])
    for copy in o_c + m_c:
        copy.wait_recv()
    mid_t, root_t, top_t = (mt[i] for i in range(3))
    outer_t = mo[...]
    root_skeleton = flip(root_t)
    skel_out[...] = root_skeleton
    grams = [exact_dot(flip(mid_t), mid_t), exact_dot(root_skeleton, root_t)]
    mid_inv, root_inv = swept(sweep([row_groups(g) for g in grams], 0, SIDE, True))
    mid_out[...] = exact_dot(exact_dot(flip(outer_t), mid_t), mid_inv)
    top_all = exact_dot(exact_dot(flip(top_t), root_t), root_inv)
    root_out[...] = jnp.where(n % 2 == 0, top_all[: SIDE // 2], top_all[SIDE // 2 :])

    half1 = x1[z]
    for copy, part in zip(then_z, range(NZ - 1)):
        copy.wait_recv()
        half1 = half1 + y1_in[part]
    half2 = x2[y]
    for copy, part in zip(then_y, range(NY - 1)):
        copy.wait_recv()
        half2 = half2 + y2_in[part]
    leaf_out[...] = exact_dot(jnp.concatenate([half1, half2], axis=0), kept[...])

    for copy in sent:
        copy.wait_send()

    @pl.when(near)
    def _():
        c_of.wait_send()
        for copy in y_of:
            copy.wait_send()

    @pl.when(special)
    def _():
        for copy in z_of:
            copy.wait_send()


COPIES = 96


def hand_over(*refs):
    count = len(refs) // 2
    for i in range(count):
        refs[count + i][...] = refs[i][...]


def per_device(front_slab, omega_codes, block_mask, leaf_pivots, mid_pivots, root_pivots):
    height, width = front_slab.shape
    samples = omega_codes.shape[1]
    vmem = pl.BlockSpec(memory_space=pltpu.VMEM)
    anywhere = pl.BlockSpec(memory_space=pl.ANY)
    share = height // (NY * NZ * NC)
    half = height // NC
    results = pl.pallas_call(
        kernel,
        out_shape=(
            jax.ShapeDtypeStruct((share, SIDE), F32),
            jax.ShapeDtypeStruct((SIDE, SIDE), F32),
            jax.ShapeDtypeStruct((SIDE // 2, SIDE), F32),
            jax.ShapeDtypeStruct((SIDE, samples), F32),
        ),
        in_specs=[anywhere, anywhere, pl.BlockSpec(memory_space=pltpu.SMEM), vmem, vmem, vmem],
        out_specs=(vmem,) * 4,
        scratch_shapes=[
            pltpu.VMEM((height, width), BF16),
            pltpu.VMEM((width, samples), jnp.int32),
            pltpu.VMEM((width, samples), BF16),
            pltpu.VMEM((NC, NY, half // NY, samples), F32),
            pltpu.VMEM((NY, half // NY, samples), F32),
            pltpu.VMEM((3, samples, SIDE), F32),
            pltpu.VMEM((3, HALF, SIDE), F32),
            pltpu.VMEM((3, HALF, SIDE), F32),
            pltpu.VMEM((NY - 1, 3, PART, SIDE), F32),
            pltpu.VMEM((3, PART, SIDE), F32),
            pltpu.VMEM((NZ, PART, SIDE), F32),
            pltpu.VMEM((NZ, 2, PART, SIDE), F32),
            pltpu.VMEM((2, PART, SIDE), F32),
            pltpu.VMEM((samples, SIDE), F32),
            pltpu.VMEM((NX, PART, SIDE), F32),
            pltpu.VMEM((2, PART, SIDE), F32),
            pltpu.VMEM((samples, SIDE), F32),
            pltpu.VMEM((3, samples, SIDE), F32),
            pltpu.VMEM((2, NY, NZ, PIECE, SIDE), F32),
            pltpu.VMEM((NY - 1, NZ, PIECE, SIDE), F32),
            pltpu.VMEM((NZ - 1, NY, PIECE, SIDE), F32),
            pltpu.VMEM((NZ, PIECE, SIDE), F32),
            pltpu.VMEM((NY, PIECE, SIDE), F32),
            pltpu.VMEM((NZ - 1, PIECE, SIDE), F32),
            pltpu.VMEM((NY - 1, PIECE, SIDE), F32),
            pltpu.VMEM((SIDE, SIDE), F32),
            pltpu.SemaphoreType.DMA((16,)),
            pltpu.SemaphoreType.DMA((COPIES,)),
            pltpu.SemaphoreType.DMA((COPIES,)),
        ],
        compiler_params=pltpu.CompilerParams(
            collective_id=0, has_side_effects=True, vmem_limit_bytes=56 << 20
        ),
    )(front_slab, omega_codes, block_mask.T, leaf_pivots, mid_pivots, root_pivots.reshape(1, SIDE))
    return pl.pallas_call(
        hand_over,
        out_shape=tuple(jax.ShapeDtypeStruct(v.shape, v.dtype) for v in results),
        in_specs=[vmem] * len(results),
        out_specs=(vmem,) * len(results),
        compiler_params=pltpu.CompilerParams(vmem_limit_bytes=56 << 20),
    )(*results)


def solution(mesh):
    return jax.shard_map(
        per_device,
        mesh=mesh,
        in_specs=(P("node", "row"), P("row", None), P("node", "row"), P("node", None), P(), P()),
        out_specs=(P(("node", "row"), None), P("node", None), P("node", None), P()),
        check_vma=False,
    )
```

```python
import jax
import jax.numpy as jnp
from jax import lax
from jax.experimental import pallas as pl
from jax.experimental.pallas import tpu as pltpu
from jax.sharding import PartitionSpec as P

F32 = jnp.float32
BF16 = jnp.bfloat16
MESH = pl.DeviceIdType.MESH
TOP = lax.Precision.HIGHEST

NX, NY, NZ, NC = 4, 4, 8, 2
SIDE = 128
SAMPLES = 384
CHUNK = 256
HALF = SAMPLES // NC
PART = HALF // NY
SPLIT = 0
PIECE = 16


def exact_dot(a, b):
    return jnp.dot(a, b, precision=TOP, preferred_element_type=F32)


def choose_dot(a, chosen):
    high = a.astype(BF16)
    rest = a - high.astype(F32)
    middle = rest.astype(BF16)
    low = (rest - middle.astype(F32)).astype(BF16)
    return sum(jnp.dot(t, chosen, preferred_element_type=F32) for t in (low, middle, high))


def flip(block):
    rows, cols = block.shape
    return jnp.concatenate(
        [
            jnp.concatenate(
                [block[i : i + SIDE, j : j + SIDE].T for i in range(0, rows, SIDE)], axis=1
            )
            for j in range(0, cols, SIDE)
        ],
        axis=0,
    )


def pivot_rows(rows, k):
    b, n = 8, SIDE
    lane = lax.broadcasted_iota(jnp.int32, (b, n), 1)
    inside = (lane >= k) & (lane < k + b)
    col = [jnp.broadcast_to(rows[:, k + j : k + j + 1], (b, n)) for j in range(b)]
    e = [[None] * b for _ in range(b)]
    for i in range(b):
        for j in range(i, b):
            e[i][j] = jnp.broadcast_to(col[j][i : i + 1, :], (b, n))
    u = [
        jnp.where(
            inside,
            jnp.where(lane == k + j, -1.0, 0.0),
            jnp.broadcast_to(rows[j : j + 1, :], (b, n)),
        )
        for j in range(b)
    ]
    d = [None] * b
    low = [[None] * b for _ in range(b)]
    for j in range(b):
        d[j] = pltpu.reciprocal(e[j][j], approx=False)
        for i in range(j + 1, b):
            low[i][j] = e[j][i] * d[j]
            for q in range(i, b):
                e[i][q] = e[i][q] - low[i][j] * e[j][q]
            u[i] = u[i] - low[i][j] * u[j]
    v = [None] * b
    for i in reversed(range(b)):
        v[i] = d[i] * u[i]
        for q in range(i + 1, b):
            v[i] = v[i] - low[q][i] * v[q]
    return v


def row_groups(matrix):
    return [matrix[8 * g : 8 * g + 8, :] for g in range(SIDE // 8)]


def swept(work):
    return [-jnp.concatenate(m, axis=0) for m in work]


def sweep(work, first, last, by_dot):
    b, n = 8, SIDE
    groups = n // b
    lane = lax.broadcasted_iota(jnp.int32, (b, n), 1)
    sub = lax.broadcasted_iota(jnp.int32, (b, n), 0)
    work = list(work)
    for k in range(first, last, b):
        own = k // b
        inside = (lane >= k) & (lane < k + b)
        pivots = [pivot_rows(m[own], k) for m in work]
        for t, m in enumerate(work):
            v = pivots[t]
            new = [None] * groups
            new[own] = v[0]
            for j in range(1, b):
                new[own] = jnp.where(sub == j, v[j], new[own])
            order = [(own + 1 + q) % groups for q in range(groups - 1)]
            if by_dot:
                update = exact_dot(jnp.concatenate(m, axis=0)[:, k : k + b], new[own])
            for at, g in enumerate(order):
                part = jnp.where(inside, 0.0, m[g])
                if by_dot and at > 0:
                    part = part - update[b * g : b * g + b]
                else:
                    for j in range(b):
                        part = part - jnp.broadcast_to(m[g][:, k + j : k + j + 1], (b, n)) * v[j]
                new[g] = part
            work[t] = new
    return work


def kernel(
    slab_hbm, codes_hbm, marks, leaf_piv, mid_piv, root_piv,
    leaf_out, mid_out, root_out, skel_out,
    slab, codes, omega, tall, tall_in, qt, cb, hb, yb, zb, rz, rzo, fo, st,
    xf, xo, mo, mt, xh, x1_in, x2_in, x1, x2, y1_in, y2_in, kept,
    load_sem, send_sem, recv_sem,
):
    n = lax.axis_index("node")
    r = lax.axis_index("row")
    y, z, c = r // (NZ * NC), (r // NC) % NZ, r % NC
    chunks = slab.shape[0] // CHUNK
    width = slab.shape[1]
    span = slab.shape[0]
    mark_width = width // marks.shape[0]

    def where_is(x_at, y_at, z_at, c_at):
        return (x_at, y_at * (NZ * NC) + z_at * NC + c_at)

    def apart(work):
        pl.when(r >= 0)(work)

    load_omega = pltpu.make_async_copy(codes_hbm, codes, load_sem.at[chunks])
    load_omega.start()
    loads = []
    for a in range(chunks):
        place = pl.ds(a * CHUNK, CHUNK)
        loads.append(
            pltpu.make_async_copy(slab_hbm.at[place], slab.at[place], load_sem.at[a])
        )
        loads[-1].start()

    sibling = where_is(n, y, z, 1 - c)
    on_y = [where_is(n, (y + d) % NY, z, c) for d in range(1, NY)]
    on_z = [where_is(n, y, (z + d) % NZ, c) for d in range(1, NZ)]
    on_x = [where_is((n + d) % NX, y, z, c) for d in range(1, NX)]
    pair = where_is(n + 1 - 2 * (n % 2), y, z, c)
    barrier = pltpu.get_barrier_semaphore()
    friends = [sibling] + on_y + on_z + on_x
    for friend in friends:
        pl.semaphore_signal(barrier, inc=1, device_id=friend, device_id_type=MESH)

    count = [0]
    sent = []

    def remote(src, dst, to):
        at = count[0]
        count[0] += 1
        return pltpu.make_async_remote_copy(
            src_ref=src, dst_ref=dst, send_sem=send_sem.at[at], recv_sem=recv_sem.at[at],
            device_id=to, device_id_type=MESH,
        )

    def go(copy):
        copy.start()
        sent.append(copy)

    lane = lax.broadcasted_iota(jnp.int32, (1, width), 1)
    column = lane + r * width
    region = jnp.where(column < NX * span, column // span, NX)
    off_leaf = (region != n).astype(F32)
    off_outer = (region // 2 != n // 2).astype(F32)
    off_far = (region == NX).astype(F32)
    mark_of = lane // mark_width

    def masked(a):
        keep = jnp.zeros_like(off_leaf)
        for b in range(marks.shape[0]):
            keep = jnp.where(mark_of == b, marks[b, a].astype(F32), keep)
        keep = (keep * off_leaf).astype(BF16)
        return slab[pl.ds(pl.multiple_of(a * CHUNK, CHUNK), CHUNK), :] * keep

    load_omega.wait()
    omega[...] = (codes[...].astype(F32) * 0.5).astype(BF16)
    piv_rows = jnp.broadcast_to(leaf_piv[0:1, :].astype(F32), (SIDE, SIDE)).T.astype(jnp.int32)
    spot = lax.broadcasted_iota(jnp.int32, (SIDE, SIDE), 1)
    picked = jnp.zeros((SIDE, width), F32)
    for a in range(chunks):
        loads[a].wait()
        pick = jnp.concatenate(
            [
                jnp.where(piv_rows == spot + (a * CHUNK + h), 1.0, 0.0)
                for h in range(0, CHUNK, SIDE)
            ],
            axis=1,
        ).astype(BF16)
        picked = picked + jnp.dot(pick, masked(a), preferred_element_type=F32)

    special = z <= 2
    near = special & (y == 0)
    qt[0] = flip(jnp.dot(picked.astype(BF16), omega[...], preferred_element_type=F32))
    pl.semaphore_wait(barrier, len(friends))

    away = pl.ds((1 - c) * HALF, HALF)
    mine = pl.ds(c * HALF, HALF)
    c_l = remote(qt.at[0, away], cb.at[0], sibling)
    c_of = remote(qt.at[pl.ds(1, 2), away], cb.at[pl.ds(1, 2)], sibling)
    go(c_l)

    @pl.when(near)
    def _():
        for i, off in ((1, off_outer), (2, off_far)):
            part = jnp.dot((picked * off).astype(BF16), omega[...], preferred_element_type=F32)
            qt[i] = flip(part)
        c_of.start()

    def tall_chunk(a):
        res = jnp.dot(masked(a), omega[...], preferred_element_type=F32)
        at_y, z0 = a // 2, (a % 2) * (CHUNK // 64)
        for i in range(CHUNK // 32):
            zz, cc = i // 2, i % 2
            rows = pl.ds(pl.multiple_of((z0 + zz) * 32, 32), 32)
            tall[cc, at_y, rows, :] = res[i * 32 : (i + 1) * 32]

    tall_copies = [remote(tall.at[1 - c, q], tall_in.at[q], sibling) for q in range(NY)]

    def tall_part(q):
        @apart
        def _():
            tall_chunk(2 * q)
            tall_chunk(2 * q + 1)

        go(tall_copies[q])

    tall_part(0)
    c_l.wait_recv()
    hb[0] = qt[0, mine, :] + cb[0]
    y_l = [remote(hb.at[0, pl.ds((y + d) % NY * PART, PART)], yb.at[d - 1, 0], on_y[d - 1]) for d in range(1, NY)]
    y_of = [
        remote(hb.at[pl.ds(1, 2), pl.ds((y + d) % NY * PART, PART)], yb.at[d - 1, pl.ds(1, 2)], on_y[d - 1])
        for d in range(1, NY)
    ]
    for d in (2, 1, 3):
        go(y_l[d - 1])

    @pl.when(near)
    def _():
        c_of.wait_recv()
        for i in (1, 2):
            hb[i] = qt[i, mine, :] + cb[i]
        for d in (2, 1, 3):
            y_of[d - 1].start()

    tall_part(1)

    own_y = pl.ds(y * PART, PART)
    for d in range(1, NY):
        y_l[d - 1].wait_recv()
    zb[0] = hb[0, own_y, :] + yb[0, 0] + yb[1, 0] + yb[2, 0]
    z_order = (4, 3, 5, 2, 6, 1, 7)
    z_l = [remote(zb.at[0], rz.at[z], on_z[d - 1]) for d in range(1, NZ)]
    z_of = [remote(zb.at[pl.ds(1, 2)], rzo.at[z], on_z[d - 1]) for d in range(1, NZ)]
    for d in z_order:
        go(z_l[d - 1])
    rz[z] = zb[0]

    @pl.when(near)
    def _():
        for i in (1, 2):
            zb[i] = hb[i, own_y, :] + yb[0, 0] + yb[1, 0] + yb[2, 0]

    for d in range(1, NY):

        @pl.when(special & (y == d))
        def _():
            y_of[d - 1].wait_recv()
            base = hb[0, own_y, :]
            for other in range(1, NY):
                if other != d:
                    base = base + yb[other - 1, 0]
            for i in (1, 2):
                zb[i] = base + yb[d - 1, i]

    @pl.when(special)
    def _():
        for d in z_order:
            z_of[d - 1].start()
        rzo[z] = zb[1:3]

    tall_part(2)
    tall_part(3)

    for d in range(1, NZ):
        z_l[d - 1].wait_recv()
    total = rz[0]
    for i in range(1, NZ):
        total = total + rz[i]
    here = c * HALF + y * PART
    st[pl.ds(here, PART), :] = total

    def rows_of(y_at):
        return pl.ds(c * HALF + y_at * PART, PART)

    def gather(view):
        along = [remote(view(y), view(y), on_y[d - 1]) for d in range(1, NY)]
        across = [remote(view((y + NY - d) % NY), view((y + NY - d) % NY), sibling) for d in range(NY)]
        return along, across

    def begin(along, across):
        for d in (2, 1, 3):
            go(along[d - 1])
        go(across[0])

    def forward(along, across):
        for d in range(1, NY):
            along[d - 1].wait_recv()
            go(across[d])

    s_y, s_c = gather(lambda y_at: st.at[rows_of(y_at)])
    begin(s_y, s_c)

    for q in range(NY):
        tall_copies[q].wait_recv()
        tall_in[q] = tall_in[q] + tall[c, q]

    for i in range(3):

        @pl.when(z != i)
        def _():
            for d in range(1, NZ):

                @pl.when((z + NZ - d) % NZ == i)
                def _():
                    z_of[d - 1].wait_recv()

    for i in range(2):
        part = rzo[0, i] + rzo[1, i] + rzo[2, i]
        for j in range(3, NZ):
            part = part + rz[j]
        fo[i] = part
    xo[n % 2] = fo[0]
    xf[n] = fo[1]
    x_o = remote(fo.at[0], xo.at[n % 2], pair)
    x_f = [remote(fo.at[1], xf.at[n], on_x[d - 1]) for d in range(1, NX)]
    go(x_f[1])
    go(x_o)
    go(x_f[0])
    go(x_f[2])
    own_part = pl.ds(here, PART)
    mo[own_part, :] = fo[0]
    o_y, o_c = gather(lambda y_at: mo.at[rows_of(y_at)])
    begin(o_y, o_c)

    forward(s_y, s_c)
    for copy in s_c:
        copy.wait_recv()
    skeleton_t = st[...]
    first_y = [remote(xh.at[0, (y + d) % NY], x1_in.at[d - 1], on_y[d - 1]) for d in range(1, NY)]
    first_z = [remote(xh.at[1, :, (z + d) % NZ], x2_in.at[d - 1], on_z[d - 1]) for d in range(1, NZ)]
    for d in (2, 1, 3, 0):
        at_y = (y + d) % NY
        cross = exact_dot(tall_in[at_y], skeleton_t)
        for i in range(NZ * 2):
            xh[i % 2, at_y, i // 2] = cross[i * PIECE : (i + 1) * PIECE]
        if d:
            go(first_y[d - 1])
    for d in z_order:
        go(first_z[d - 1])

    from_sub = lax.broadcasted_iota(jnp.int32, (2 * SIDE, SIDE), 0)

    def chooser(row):
        return jnp.where(from_sub == row, 1.0, 0.0).astype(BF16)

    parent = n // 2
    choose_mid = [chooser(mid_piv[q : q + 1, :]) for q in range(2)]
    choose_own = jnp.where(parent == 0, choose_mid[0], choose_mid[1])
    @apart
    def _():
        work = [row_groups(exact_dot(flip(st[...]), st[...]))]
        kept[...] = jnp.concatenate(sweep(work, 0, SPLIT, False)[0], axis=0)

    x_o.wait_recv()
    for d in range(1, NX):
        x_f[d - 1].wait_recv()
    upper = [
        choose_dot(jnp.concatenate([xf[2 * q], xf[2 * q + 1]], axis=1), choose_mid[q])
        for q in range(2)
    ]
    mt[0, own_part, :] = choose_dot(jnp.concatenate([xo[0], xo[1]], axis=1), choose_own)
    mt[1, own_part, :] = choose_dot(jnp.concatenate(upper, axis=1), chooser(root_piv[0:1, :]))
    mt[2, own_part, :] = jnp.where(parent == 0, upper[0], upper[1])
    m_y, m_c = gather(lambda y_at: mt.at[:, rows_of(y_at)])
    begin(m_y, m_c)
    forward(o_y, o_c)

    @apart
    def _():
        kept[...] = swept(sweep([row_groups(kept[...])], SPLIT, SIDE, False))[0]


    for copy in first_y:
        copy.wait_recv()
    x1[...] = xh[0, y] + x1_in[0] + x1_in[1] + x1_in[2]
    then_z = [remote(x1.at[(z + d) % NZ], y1_in.at[d - 1], on_z[d - 1]) for d in range(1, NZ)]
    for d in z_order:
        go(then_z[d - 1])

    forward(m_y, m_c)
    for copy in first_z:
        copy.wait_recv()
    total2 = xh[1, :, z]
    for d in range(1, NZ):
        total2 = total2 + x2_in[d - 1]
    x2[...] = total2
    then_y = [remote(x2.at[(y + d) % NY], y2_in.at[d - 1], on_y[d - 1]) for d in range(1, NY)]
    for d in (2, 1, 3):
        go(then_y[d - 1])
    for copy in o_c + m_c:
        copy.wait_recv()
    mid_t, root_t, top_t = (mt[i] for i in range(3))
    outer_t = mo[...]
    root_skeleton = flip(root_t)
    skel_out[...] = root_skeleton
    grams = [exact_dot(flip(mid_t), mid_t), exact_dot(root_skeleton, root_t)]
    mid_inv, root_inv = swept(sweep([row_groups(g) for g in grams], 0, SIDE, True))
    mid_out[...] = exact_dot(exact_dot(flip(outer_t), mid_t), mid_inv)
    top_all = exact_dot(exact_dot(flip(top_t), root_t), root_inv)
    root_out[...] = jnp.where(n % 2 == 0, top_all[: SIDE // 2], top_all[SIDE // 2 :])

    half1 = x1[z]
    for copy, part in zip(then_z, range(NZ - 1)):
        copy.wait_recv()
        half1 = half1 + y1_in[part]
    half2 = x2[y]
    for copy, part in zip(then_y, range(NY - 1)):
        copy.wait_recv()
        half2 = half2 + y2_in[part]
    leaf_out[...] = exact_dot(jnp.concatenate([half1, half2], axis=0), kept[...])

    for copy in sent:
        copy.wait_send()

    @pl.when(near)
    def _():
        c_of.wait_send()
        for copy in y_of:
            copy.wait_send()

    @pl.when(special)
    def _():
        for copy in z_of:
            copy.wait_send()


COPIES = 96


def hand_over(*refs):
    count = len(refs) // 2
    for i in range(count):
        refs[count + i][...] = refs[i][...]


def per_device(front_slab, omega_codes, block_mask, leaf_pivots, mid_pivots, root_pivots):
    height, width = front_slab.shape
    samples = omega_codes.shape[1]
    vmem = pl.BlockSpec(memory_space=pltpu.VMEM)
    anywhere = pl.BlockSpec(memory_space=pl.ANY)
    share = height // (NY * NZ * NC)
    half = height // NC
    results = pl.pallas_call(
        kernel,
        out_shape=(
            jax.ShapeDtypeStruct((share, SIDE), F32),
            jax.ShapeDtypeStruct((SIDE, SIDE), F32),
            jax.ShapeDtypeStruct((SIDE // 2, SIDE), F32),
            jax.ShapeDtypeStruct((SIDE, samples), F32),
        ),
        in_specs=[anywhere, anywhere, pl.BlockSpec(memory_space=pltpu.SMEM), vmem, vmem, vmem],
        out_specs=(vmem,) * 4,
        scratch_shapes=[
            pltpu.VMEM((height, width), BF16),
            pltpu.VMEM((width, samples), jnp.int32),
            pltpu.VMEM((width, samples), BF16),
            pltpu.VMEM((NC, NY, half // NY, samples), F32),
            pltpu.VMEM((NY, half // NY, samples), F32),
            pltpu.VMEM((3, samples, SIDE), F32),
            pltpu.VMEM((3, HALF, SIDE), F32),
            pltpu.VMEM((3, HALF, SIDE), F32),
            pltpu.VMEM((NY - 1, 3, PART, SIDE), F32),
            pltpu.VMEM((3, PART, SIDE), F32),
            pltpu.VMEM((NZ, PART, SIDE), F32),
            pltpu.VMEM((NZ, 2, PART, SIDE), F32),
            pltpu.VMEM((2, PART, SIDE), F32),
            pltpu.VMEM((samples, SIDE), F32),
            pltpu.VMEM((NX, PART, SIDE), F32),
            pltpu.VMEM((2, PART, SIDE), F32),
            pltpu.VMEM((samples, SIDE), F32),
            pltpu.VMEM((3, samples, SIDE), F32),
            pltpu.VMEM((2, NY, NZ, PIECE, SIDE), F32),
            pltpu.VMEM((NY - 1, NZ, PIECE, SIDE), F32),
            pltpu.VMEM((NZ - 1, NY, PIECE, SIDE), F32),
            pltpu.VMEM((NZ, PIECE, SIDE), F32),
            pltpu.VMEM((NY, PIECE, SIDE), F32),
            pltpu.VMEM((NZ - 1, PIECE, SIDE), F32),
            pltpu.VMEM((NY - 1, PIECE, SIDE), F32),
            pltpu.VMEM((SIDE, SIDE), F32),
            pltpu.SemaphoreType.DMA((16,)),
            pltpu.SemaphoreType.DMA((COPIES,)),
            pltpu.SemaphoreType.DMA((COPIES,)),
        ],
        compiler_params=pltpu.CompilerParams(
            collective_id=0, has_side_effects=True, vmem_limit_bytes=56 << 20
        ),
    )(front_slab, omega_codes, block_mask.T, leaf_pivots, mid_pivots, root_pivots.reshape(1, SIDE))
    return pl.pallas_call(
        hand_over,
        out_shape=tuple(jax.ShapeDtypeStruct(v.shape, v.dtype) for v in results),
        in_specs=[vmem] * len(results),
        out_specs=(vmem,) * len(results),
        compiler_params=pltpu.CompilerParams(vmem_limit_bytes=56 << 20),
    )(*results)


def solution(mesh):
    return jax.shard_map(
        per_device,
        mesh=mesh,
        in_specs=(P("node", "row"), P("row", None), P("node", "row"), P("node", None), P(), P()),
        out_specs=(P(("node", "row"), None), P("node", None), P("node", None), P()),
        check_vma=False,
    )
```

```python
import jax
import jax.numpy as jnp
from jax import lax
from jax.experimental import pallas as pl
from jax.experimental.pallas import tpu as pltpu
from jax.sharding import PartitionSpec as P

F32 = jnp.float32
BF16 = jnp.bfloat16
MESH = pl.DeviceIdType.MESH
TOP = lax.Precision.HIGHEST

NX, NY, NZ, NC = 4, 4, 8, 2
SIDE = 128
SAMPLES = 384
CHUNK = 256
HALF = SAMPLES // NC
PART = HALF // NY
SPLIT = 0
PIECE = 16


def exact_dot(a, b):
    return jnp.dot(a, b, precision=TOP, preferred_element_type=F32)


def choose_dot(a, chosen):
    high = a.astype(BF16)
    rest = a - high.astype(F32)
    middle = rest.astype(BF16)
    low = (rest - middle.astype(F32)).astype(BF16)
    return sum(jnp.dot(t, chosen, preferred_element_type=F32) for t in (low, middle, high))


def flip(block):
    rows, cols = block.shape
    return jnp.concatenate(
        [
            jnp.concatenate(
                [block[i : i + SIDE, j : j + SIDE].T for i in range(0, rows, SIDE)], axis=1
            )
            for j in range(0, cols, SIDE)
        ],
        axis=0,
    )


def pivot_rows(rows, k):
    b, n = 8, SIDE
    lane = lax.broadcasted_iota(jnp.int32, (b, n), 1)
    inside = (lane >= k) & (lane < k + b)
    col = [jnp.broadcast_to(rows[:, k + j : k + j + 1], (b, n)) for j in range(b)]
    e = [[None] * b for _ in range(b)]
    for i in range(b):
        for j in range(i, b):
            e[i][j] = jnp.broadcast_to(col[j][i : i + 1, :], (b, n))
    u = [
        jnp.where(
            inside,
            jnp.where(lane == k + j, -1.0, 0.0),
            jnp.broadcast_to(rows[j : j + 1, :], (b, n)),
        )
        for j in range(b)
    ]
    d = [None] * b
    low = [[None] * b for _ in range(b)]
    for j in range(b):
        d[j] = pltpu.reciprocal(e[j][j], approx=False)
        for i in range(j + 1, b):
            low[i][j] = e[j][i] * d[j]
            for q in range(i, b):
                e[i][q] = e[i][q] - low[i][j] * e[j][q]
            u[i] = u[i] - low[i][j] * u[j]
    v = [None] * b
    for i in reversed(range(b)):
        v[i] = d[i] * u[i]
        for q in range(i + 1, b):
            v[i] = v[i] - low[q][i] * v[q]
    return v


def row_groups(matrix):
    return [matrix[8 * g : 8 * g + 8, :] for g in range(SIDE // 8)]


def swept(work):
    return [-jnp.concatenate(m, axis=0) for m in work]


def sweep(work, first, last, by_dot):
    b, n = 8, SIDE
    groups = n // b
    lane = lax.broadcasted_iota(jnp.int32, (b, n), 1)
    sub = lax.broadcasted_iota(jnp.int32, (b, n), 0)
    work = list(work)
    for k in range(first, last, b):
        own = k // b
        inside = (lane >= k) & (lane < k + b)
        pivots = [pivot_rows(m[own], k) for m in work]
        for t, m in enumerate(work):
            v = pivots[t]
            new = [None] * groups
            new[own] = v[0]
            for j in range(1, b):
                new[own] = jnp.where(sub == j, v[j], new[own])
            order = [(own + 1 + q) % groups for q in range(groups - 1)]
            if by_dot:
                update = exact_dot(jnp.concatenate(m, axis=0)[:, k : k + b], new[own])
            for at, g in enumerate(order):
                part = jnp.where(inside, 0.0, m[g])
                if by_dot and at > 0:
                    part = part - update[b * g : b * g + b]
                else:
                    for j in range(b):
                        part = part - jnp.broadcast_to(m[g][:, k + j : k + j + 1], (b, n)) * v[j]
                new[g] = part
            work[t] = new
    return work


def kernel(
    slab_hbm, codes_hbm, marks, leaf_piv, mid_piv, root_piv,
    leaf_out, mid_out, root_out, skel_out,
    slab, codes, omega, tall, tall_in, qt, cb, hb, yb, zb, rz, rzo, fo, st,
    xf, xo, mo, mt, xh, x1_in, x2_in, x1, x2, y1_in, y2_in, kept,
    load_sem, send_sem, recv_sem,
):
    n = lax.axis_index("node")
    r = lax.axis_index("row")
    y, z, c = r // (NZ * NC), (r // NC) % NZ, r % NC
    chunks = slab.shape[0] // CHUNK
    width = slab.shape[1]
    span = slab.shape[0]
    mark_width = width // marks.shape[0]

    def where_is(x_at, y_at, z_at, c_at):
        return (x_at, y_at * (NZ * NC) + z_at * NC + c_at)

    def apart(work):
        pl.when(r >= 0)(work)

    load_omega = pltpu.make_async_copy(codes_hbm, codes, load_sem.at[chunks])
    load_omega.start()
    loads = []
    for a in range(chunks):
        place = pl.ds(a * CHUNK, CHUNK)
        loads.append(
            pltpu.make_async_copy(slab_hbm.at[place], slab.at[place], load_sem.at[a])
        )
        loads[-1].start()

    sibling = where_is(n, y, z, 1 - c)
    on_y = [where_is(n, (y + d) % NY, z, c) for d in range(1, NY)]
    on_z = [where_is(n, y, (z + d) % NZ, c) for d in range(1, NZ)]
    on_x = [where_is((n + d) % NX, y, z, c) for d in range(1, NX)]
    pair = where_is(n + 1 - 2 * (n % 2), y, z, c)
    barrier = pltpu.get_barrier_semaphore()
    friends = [sibling] + on_y + on_z + on_x
    for friend in friends:
        pl.semaphore_signal(barrier, inc=1, device_id=friend, device_id_type=MESH)

    count = [0]
    sent = []

    def remote(src, dst, to):
        at = count[0]
        count[0] += 1
        return pltpu.make_async_remote_copy(
            src_ref=src, dst_ref=dst, send_sem=send_sem.at[at], recv_sem=recv_sem.at[at],
            device_id=to, device_id_type=MESH,
        )

    def go(copy):
        copy.start()
        sent.append(copy)

    lane = lax.broadcasted_iota(jnp.int32, (1, width), 1)
    column = lane + r * width
    region = jnp.where(column < NX * span, column // span, NX)
    off_leaf = (region != n).astype(F32)
    off_outer = (region // 2 != n // 2).astype(F32)
    off_far = (region == NX).astype(F32)
    mark_of = lane // mark_width

    def masked(a):
        keep = jnp.zeros_like(off_leaf)
        for b in range(marks.shape[0]):
            keep = jnp.where(mark_of == b, marks[b, a].astype(F32), keep)
        keep = (keep * off_leaf).astype(BF16)
        return slab[pl.ds(pl.multiple_of(a * CHUNK, CHUNK), CHUNK), :] * keep

    load_omega.wait()
    omega[...] = (codes[...].astype(F32) * 0.5).astype(BF16)
    piv_rows = jnp.broadcast_to(leaf_piv[0:1, :].astype(F32), (SIDE, SIDE)).T.astype(jnp.int32)
    spot = lax.broadcasted_iota(jnp.int32, (SIDE, SIDE), 1)
    picked = jnp.zeros((SIDE, width), F32)
    for a in range(chunks):
        loads[a].wait()
        pick = jnp.concatenate(
            [
                jnp.where(piv_rows == spot + (a * CHUNK + h), 1.0, 0.0)
                for h in range(0, CHUNK, SIDE)
            ],
            axis=1,
        ).astype(BF16)
        picked = picked + jnp.dot(pick, masked(a), preferred_element_type=F32)

    special = z <= 2
    near = special & (y == 0)
    qt[0] = flip(jnp.dot(picked.astype(BF16), omega[...], preferred_element_type=F32))
    pl.semaphore_wait(barrier, len(friends))

    away = pl.ds((1 - c) * HALF, HALF)
    mine = pl.ds(c * HALF, HALF)
    c_l = remote(qt.at[0, away], cb.at[0], sibling)
    c_of = remote(qt.at[pl.ds(1, 2), away], cb.at[pl.ds(1, 2)], sibling)
    go(c_l)

    @pl.when(near)
    def _():
        for i, off in ((1, off_outer), (2, off_far)):
            part = jnp.dot((picked * off).astype(BF16), omega[...], preferred_element_type=F32)
            qt[i] = flip(part)
        c_of.start()

    def tall_chunk(a):
        res = jnp.dot(masked(a), omega[...], preferred_element_type=F32)
        at_y, z0 = a // 2, (a % 2) * (CHUNK // 64)
        for i in range(CHUNK // 32):
            zz, cc = i // 2, i % 2
            rows = pl.ds(pl.multiple_of((z0 + zz) * 32, 32), 32)
            tall[cc, at_y, rows, :] = res[i * 32 : (i + 1) * 32]

    tall_copies = [remote(tall.at[1 - c, q], tall_in.at[q], sibling) for q in range(NY)]

    def tall_part(q):
        @apart
        def _():
            tall_chunk(2 * q)
            tall_chunk(2 * q + 1)

        go(tall_copies[q])

    tall_part(0)
    c_l.wait_recv()
    hb[0] = qt[0, mine, :] + cb[0]
    y_l = [remote(hb.at[0, pl.ds((y + d) % NY * PART, PART)], yb.at[d - 1, 0], on_y[d - 1]) for d in range(1, NY)]
    y_of = [
        remote(hb.at[pl.ds(1, 2), pl.ds((y + d) % NY * PART, PART)], yb.at[d - 1, pl.ds(1, 2)], on_y[d - 1])
        for d in range(1, NY)
    ]
    for d in (2, 1, 3):
        go(y_l[d - 1])

    @pl.when(near)
    def _():
        c_of.wait_recv()
        for i in (1, 2):
            hb[i] = qt[i, mine, :] + cb[i]
        for d in (2, 1, 3):
            y_of[d - 1].start()

    tall_part(1)

    own_y = pl.ds(y * PART, PART)
    for d in range(1, NY):
        y_l[d - 1].wait_recv()
    zb[0] = hb[0, own_y, :] + yb[0, 0] + yb[1, 0] + yb[2, 0]
    z_order = (4, 3, 5, 2, 6, 1, 7)
    z_l = [remote(zb.at[0], rz.at[z], on_z[d - 1]) for d in range(1, NZ)]
    z_of = [remote(zb.at[pl.ds(1, 2)], rzo.at[z], on_z[d - 1]) for d in range(1, NZ)]
    for d in z_order:
        go(z_l[d - 1])
    rz[z] = zb[0]

    @pl.when(near)
    def _():
        for i in (1, 2):
            zb[i] = hb[i, own_y, :] + yb[0, 0] + yb[1, 0] + yb[2, 0]

    for d in range(1, NY):

        @pl.when(special & (y == d))
        def _():
            y_of[d - 1].wait_recv()
            base = hb[0, own_y, :]
            for other in range(1, NY):
                if other != d:
                    base = base + yb[other - 1, 0]
            for i in (1, 2):
                zb[i] = base + yb[d - 1, i]

    @pl.when(special)
    def _():
        for d in z_order:
            z_of[d - 1].start()
        rzo[z] = zb[1:3]

    tall_part(2)
    tall_part(3)

    for d in range(1, NZ):
        z_l[d - 1].wait_recv()
    total = rz[0]
    for i in range(1, NZ):
        total = total + rz[i]
    here = c * HALF + y * PART
    st[pl.ds(here, PART), :] = total

    def rows_of(y_at):
        return pl.ds(c * HALF + y_at * PART, PART)

    def gather(view):
        along = [remote(view(y), view(y), on_y[d - 1]) for d in range(1, NY)]
        across = [remote(view((y + NY - d) % NY), view((y + NY - d) % NY), sibling) for d in range(NY)]
        return along, across

    def begin(along, across):
        for d in (2, 1, 3):
            go(along[d - 1])
        go(across[0])

    def forward(along, across):
        for d in range(1, NY):
            along[d - 1].wait_recv()
            go(across[d])

    s_y, s_c = gather(lambda y_at: st.at[rows_of(y_at)])
    begin(s_y, s_c)

    for q in range(NY):
        tall_copies[q].wait_recv()
        tall_in[q] = tall_in[q] + tall[c, q]

    for i in range(3):

        @pl.when(z != i)
        def _():
            for d in range(1, NZ):

                @pl.when((z + NZ - d) % NZ == i)
                def _():
                    z_of[d - 1].wait_recv()

    for i in range(2):
        part = rzo[0, i] + rzo[1, i] + rzo[2, i]
        for j in range(3, NZ):
            part = part + rz[j]
        fo[i] = part
    xo[n % 2] = fo[0]
    xf[n] = fo[1]
    x_o = remote(fo.at[0], xo.at[n % 2], pair)
    x_f = [remote(fo.at[1], xf.at[n], on_x[d - 1]) for d in range(1, NX)]
    go(x_f[1])
    go(x_o)
    go(x_f[0])
    go(x_f[2])
    own_part = pl.ds(here, PART)
    mo[own_part, :] = fo[0]
    o_y, o_c = gather(lambda y_at: mo.at[rows_of(y_at)])
    begin(o_y, o_c)

    forward(s_y, s_c)
    for copy in s_c:
        copy.wait_recv()
    skeleton_t = st[...]
    first_y = [remote(xh.at[0, (y + d) % NY], x1_in.at[d - 1], on_y[d - 1]) for d in range(1, NY)]
    first_z = [remote(xh.at[1, :, (z + d) % NZ], x2_in.at[d - 1], on_z[d - 1]) for d in range(1, NZ)]
    for d in (2, 1, 3, 0):
        at_y = (y + d) % NY
        cross = exact_dot(tall_in[at_y], skeleton_t)
        for i in range(NZ * 2):
            xh[i % 2, at_y, i // 2] = cross[i * PIECE : (i + 1) * PIECE]
        if d:
            go(first_y[d - 1])
    for d in z_order:
        go(first_z[d - 1])

    from_sub = lax.broadcasted_iota(jnp.int32, (2 * SIDE, SIDE), 0)

    def chooser(row):
        return jnp.where(from_sub == row, 1.0, 0.0).astype(BF16)

    parent = n // 2
    choose_mid = [chooser(mid_piv[q : q + 1, :]) for q in range(2)]
    choose_own = jnp.where(parent == 0, choose_mid[0], choose_mid[1])
    @apart
    def _():
        work = [row_groups(exact_dot(flip(st[...]), st[...]))]
        kept[...] = jnp.concatenate(sweep(work, 0, SPLIT, False)[0], axis=0)

    x_o.wait_recv()
    for d in range(1, NX):
        x_f[d - 1].wait_recv()
    upper = [
        choose_dot(jnp.concatenate([xf[2 * q], xf[2 * q + 1]], axis=1), choose_mid[q])
        for q in range(2)
    ]
    mt[0, own_part, :] = choose_dot(jnp.concatenate([xo[0], xo[1]], axis=1), choose_own)
    mt[1, own_part, :] = choose_dot(jnp.concatenate(upper, axis=1), chooser(root_piv[0:1, :]))
    mt[2, own_part, :] = jnp.where(parent == 0, upper[0], upper[1])
    m_y, m_c = gather(lambda y_at: mt.at[:, rows_of(y_at)])
    begin(m_y, m_c)
    forward(o_y, o_c)

    @apart
    def _():
        kept[...] = swept(sweep([row_groups(kept[...])], SPLIT, SIDE, False))[0]


    forward(m_y, m_c)
    for copy in first_y:
        copy.wait_recv()
    x1[...] = xh[0, y] + x1_in[0] + x1_in[1] + x1_in[2]
    then_z = [remote(x1.at[(z + d) % NZ], y1_in.at[d - 1], on_z[d - 1]) for d in range(1, NZ)]
    for d in z_order:
        go(then_z[d - 1])

    for copy in first_z:
        copy.wait_recv()
    total2 = xh[1, :, z]
    for d in range(1, NZ):
        total2 = total2 + x2_in[d - 1]
    x2[...] = total2
    then_y = [remote(x2.at[(y + d) % NY], y2_in.at[d - 1], on_y[d - 1]) for d in range(1, NY)]
    for d in (2, 1, 3):
        go(then_y[d - 1])
    for copy in o_c + m_c:
        copy.wait_recv()
    mid_t, root_t, top_t = (mt[i] for i in range(3))
    outer_t = mo[...]
    root_skeleton = flip(root_t)
    skel_out[...] = root_skeleton
    grams = [exact_dot(flip(mid_t), mid_t), exact_dot(root_skeleton, root_t)]
    mid_inv, root_inv = swept(sweep([row_groups(g) for g in grams], 0, SIDE, True))
    mid_out[...] = exact_dot(exact_dot(flip(outer_t), mid_t), mid_inv)
    top_all = exact_dot(exact_dot(flip(top_t), root_t), root_inv)
    root_out[...] = jnp.where(n % 2 == 0, top_all[: SIDE // 2], top_all[SIDE // 2 :])

    half1 = x1[z]
    for copy, part in zip(then_z, range(NZ - 1)):
        copy.wait_recv()
        half1 = half1 + y1_in[part]
    half2 = x2[y]
    for copy, part in zip(then_y, range(NY - 1)):
        copy.wait_recv()
        half2 = half2 + y2_in[part]
    leaf_out[...] = exact_dot(jnp.concatenate([half1, half2], axis=0), kept[...])

    for copy in sent:
        copy.wait_send()

    @pl.when(near)
    def _():
        c_of.wait_send()
        for copy in y_of:
            copy.wait_send()

    @pl.when(special)
    def _():
        for copy in z_of:
            copy.wait_send()


COPIES = 96


def hand_over(*refs):
    count = len(refs) // 2
    for i in range(count):
        refs[count + i][...] = refs[i][...]


def per_device(front_slab, omega_codes, block_mask, leaf_pivots, mid_pivots, root_pivots):
    height, width = front_slab.shape
    samples = omega_codes.shape[1]
    vmem = pl.BlockSpec(memory_space=pltpu.VMEM)
    anywhere = pl.BlockSpec(memory_space=pl.ANY)
    share = height // (NY * NZ * NC)
    half = height // NC
    results = pl.pallas_call(
        kernel,
        out_shape=(
            jax.ShapeDtypeStruct((share, SIDE), F32),
            jax.ShapeDtypeStruct((SIDE, SIDE), F32),
            jax.ShapeDtypeStruct((SIDE // 2, SIDE), F32),
            jax.ShapeDtypeStruct((SIDE, samples), F32),
        ),
        in_specs=[anywhere, anywhere, pl.BlockSpec(memory_space=pltpu.SMEM), vmem, vmem, vmem],
        out_specs=(vmem,) * 4,
        scratch_shapes=[
            pltpu.VMEM((height, width), BF16),
            pltpu.VMEM((width, samples), jnp.int32),
            pltpu.VMEM((width, samples), BF16),
            pltpu.VMEM((NC, NY, half // NY, samples), F32),
            pltpu.VMEM((NY, half // NY, samples), F32),
            pltpu.VMEM((3, samples, SIDE), F32),
            pltpu.VMEM((3, HALF, SIDE), F32),
            pltpu.VMEM((3, HALF, SIDE), F32),
            pltpu.VMEM((NY - 1, 3, PART, SIDE), F32),
            pltpu.VMEM((3, PART, SIDE), F32),
            pltpu.VMEM((NZ, PART, SIDE), F32),
            pltpu.VMEM((NZ, 2, PART, SIDE), F32),
            pltpu.VMEM((2, PART, SIDE), F32),
            pltpu.VMEM((samples, SIDE), F32),
            pltpu.VMEM((NX, PART, SIDE), F32),
            pltpu.VMEM((2, PART, SIDE), F32),
            pltpu.VMEM((samples, SIDE), F32),
            pltpu.VMEM((3, samples, SIDE), F32),
            pltpu.VMEM((2, NY, NZ, PIECE, SIDE), F32),
            pltpu.VMEM((NY - 1, NZ, PIECE, SIDE), F32),
            pltpu.VMEM((NZ - 1, NY, PIECE, SIDE), F32),
            pltpu.VMEM((NZ, PIECE, SIDE), F32),
            pltpu.VMEM((NY, PIECE, SIDE), F32),
            pltpu.VMEM((NZ - 1, PIECE, SIDE), F32),
            pltpu.VMEM((NY - 1, PIECE, SIDE), F32),
            pltpu.VMEM((SIDE, SIDE), F32),
            pltpu.SemaphoreType.DMA((16,)),
            pltpu.SemaphoreType.DMA((COPIES,)),
            pltpu.SemaphoreType.DMA((COPIES,)),
        ],
        compiler_params=pltpu.CompilerParams(
            collective_id=0, has_side_effects=True, vmem_limit_bytes=56 << 20
        ),
    )(front_slab, omega_codes, block_mask.T, leaf_pivots, mid_pivots, root_pivots.reshape(1, SIDE))
    return pl.pallas_call(
        hand_over,
        out_shape=tuple(jax.ShapeDtypeStruct(v.shape, v.dtype) for v in results),
        in_specs=[vmem] * len(results),
        out_specs=(vmem,) * len(results),
        compiler_params=pltpu.CompilerParams(vmem_limit_bytes=56 << 20),
    )(*results)


def solution(mesh):
    return jax.shard_map(
        per_device,
        mesh=mesh,
        in_specs=(P("node", "row"), P("row", None), P("node", "row"), P("node", None), P(), P()),
        out_specs=(P(("node", "row"), None), P("node", None), P("node", None), P()),
        check_vma=False,
    )
```
